32 devices in a mesh: parts: 2 (over y), wide: 8 (over z, x), tp: 2 (over core).
Axes of the slice: x: 2, y: 2, z: 4, core: 2. Of those that a mesh axis runs over, the one named last changes fastest.
Arguments:
- queries: bfloat16 [16, 3, 8192], P(('parts', 'wide'), None, 'tp'), parts along dimension 0, may hold values from -6 to 6
- cache_kv: bfloat16 [2, 32, 1024, 1024], P(None, ('parts', 'wide'), None, 'tp'), parts along dimension 1, may hold values from -6 to 6
- fresh_kv: bfloat16 [2, 16, 3, 1024], P(None, ('parts', 'wide'), None, 'tp'), parts along dimension 1, may hold values from -6 to 6
- ctx_len: int32 [32], P(('parts', 'wide')), parts along dimension 0, may hold values from 1 to 1024, 8711 in all
- prefill: bfloat16 [2, 16, 2048, 1024], P(None, ('parts', 'wide'), None, 'tp'), parts along dimension 1, may hold values from -6 to 6
- prefill_scale: bfloat16 [2, 16, 2048, 8], P(None, ('parts', 'wide'), None, 'tp'), parts along dimension 1, may hold values from 0.25 to 4
- new_group: int32 [16], P('parts'), parts along dimension 0, may hold values from 0 to 7, as said below
- new_pages: int32 [16], P('parts'), parts along dimension 0, may hold values from 1 to 128, 579 in all
Outputs:
- attended: bfloat16 [16, 3, 8192], P(('parts', 'wide'), None, 'tp'), parts along dimension 0
- handed_kv: bfloat16 [2, 16, 1, 2048, 1024], P(None, ('parts', 'wide'), None, None, 'tp'), parts along dimension 1
The draws below stay inside these ranges and needn't reach their ends.
There are 2 independent parts, one for each index of `parts`. The reference program is written for one: setup_inputs(seed, part) draws one part's arguments, and reference() takes and returns one part's arrays. A program takes and returns all parts, laid end to end along the dimension named above; each array names one. Nothing has to cross between parts.
Inputs may be any that keep to these rules, and one draw needn't show every extreme that they name: `new_group`: every decode group receives exactly 1 new requests. `ctx_len`: cached positions of a resident request; at least one. A new request's prompt has new_pages * 16 positions; the rest of its rows in prefill are unused.
All inputs are finite; a program needn't handle non-finite values. No bound on the sum of `ctx_len` on one device may be relied on, other than what follows from the above.
Results may differ from the reference program's by a relative error of at most 0.008.
Values may be sent and summed in bfloat16 or wider, within the bound.
A program may use at most 128 MiB of HBM per device.

```python
import math
import jax
import jax.numpy as jnp
import numpy as np
from jax import lax

QH = 64
KVH = 8
HD = 128
ROWS_GRP = 2
CTX = 1024
NEW_GRP = 1
PROMPT = 2048
PAGE = 16
ROWS = 16
NEW = 8
SLOTS = 3
N_WIDE = 8


def group_list(key):
    key = jax.random.fold_in(key, 103)
    shuffled = jax.random.permutation(key, jnp.arange(NEW, dtype=jnp.int32))
    return (shuffled // NEW_GRP).astype(jnp.int32)


def draw_new_group(key, part):
    return group_list(key)


def draw_queries(key, part):
    key = jax.random.fold_in(key, 1)
    full_shape = (N_WIDE, SLOTS, QH * HD)
    return jax.random.truncated_normal(key, -4.0, 4.0, full_shape, jnp.float32).astype(jnp.bfloat16)


def draw_cache_kv(key, part):
    key = jax.random.fold_in(key, 2)
    full_shape = (2, ROWS, CTX, KVH * HD)
    return jax.random.truncated_normal(key, -4.0, 4.0, full_shape, jnp.float32).astype(jnp.bfloat16)


def draw_prefill(key, part):
    key = jax.random.fold_in(key, 3)
    full_shape = (2, NEW, PROMPT, KVH * HD)
    return jax.random.truncated_normal(key, -4.0, 4.0, full_shape, jnp.float32).astype(jnp.bfloat16)


def draw_prefill_scale(key, part):
    key = jax.random.fold_in(key, 4)
    full_shape = (2, NEW, PROMPT, KVH)
    return jnp.exp(jax.random.uniform(key, full_shape, jnp.float32, math.log(0.25), math.log(4.0))).astype(jnp.bfloat16)


def level_of(key, shape, shards, low, high):
    gain, own = 1.0, jax.random.fold_in(key, 6)
    for position, parts in shards:
        draws = jnp.exp(jax.random.uniform(jax.random.fold_in(own, position), (parts,), jnp.float32, low / len(shards), high / len(shards)))
        gain = gain * jnp.repeat(draws, shape[position] // parts).reshape([-1 if axis == position else 1 for axis in range(len(shape))])
    return gain


def profile(count, total, bound, slope):
    loads = [(1 << 20) // math.isqrt(grade ** slope) + 1 for grade in range(2, count + 1)]
    surplus, holding = total - bound - (count - 1), [1] * (count - 1)
    while surplus > 0:
        movable = [i for i in range(count - 1) if holding[i] < bound]
        whole, budget = sum([loads[i] for i in movable]), surplus
        for i in movable:
            addition = min(bound - holding[i], max(1, budget * loads[i] // whole), surplus)
            holding[i] = holding[i] + addition
            surplus = surplus - addition
    return np.array([bound] + holding)


def ragged_sizes(rng, number_of, total, bound, lean):
    if number_of == 2:
        one = jax.random.randint(rng, (), max(1, total - bound), min(bound, total - 1) + 1)
        return jnp.stack([one, total - one])
    tallies = jnp.asarray(profile(number_of, total, bound, lean), jnp.int32)
    pairs = (number_of - 1) // 2
    donor, receiver = tallies[1:1 + 2 * pairs:2], tallies[2:2 + 2 * pairs:2]
    slack = jnp.minimum(donor - 1, bound - receiver)
    passed = jax.random.randint(jax.random.fold_in(rng, 1), (pairs,), 0, 1 << 20) % (slack + 1)
    tallies = tallies.at[1:1 + 2 * pairs:2].set(donor - passed).at[2:2 + 2 * pairs:2].set(receiver + passed)
    return tallies[jax.random.permutation(jax.random.fold_in(rng, 2), number_of)]


def centred(rng, extent, scale, most, cuts=(), held_as=jnp.bfloat16):
    entries = scale * jax.random.normal(rng, extent, jnp.float32)
    if cuts:
        entries = entries * level_of(rng, extent, cuts, -0.22, 0.18)
    return jnp.clip(entries, -most, most).astype(held_as)


def setup_inputs(seed: int = 0, part: int = 0) -> dict:
    splits = jax.random.split(jax.random.key(seed), 9)
    own_keys = jax.random.split(jax.random.fold_in(splits[8], part), 9)
    return {
        "queries": draw_queries(jax.random.fold_in(jax.random.fold_in(splits[8], part), 71), part),
        "cache_kv": draw_cache_kv(jax.random.fold_in(jax.random.fold_in(splits[8], part), 71), part),
        "fresh_kv": centred(own_keys[2], (2, N_WIDE, SLOTS, KVH * HD), 1.0, 6.0, ((1, 8), (3, 2))),
        "ctx_len": ragged_sizes(own_keys[3], ROWS, (ROWS - 1) + CTX + (ROWS - 1) * (CTX - 1) // 2, CTX, 1).astype(jnp.int32),
        "prefill": draw_prefill(jax.random.fold_in(jax.random.fold_in(splits[8], part), 71), part),
        "prefill_scale": draw_prefill_scale(jax.random.fold_in(jax.random.fold_in(splits[8], part), 71), part),
        "new_group": draw_new_group(jax.random.fold_in(jax.random.fold_in(splits[8], part), 71), part),
        "new_pages": ragged_sizes(own_keys[7], NEW, (NEW - 1) + PROMPT // PAGE + (NEW - 1) * (PROMPT // PAGE - 1) // 2, PROMPT // PAGE, 1).astype(jnp.int32),
    }


NEG_FILL = -1e+30
HIGHEST = lax.Precision.HIGHEST

def group_ranks(groups):
    request_ids = jnp.arange(groups.shape[0], dtype=jnp.int32)
    earlier = (groups[None, :] == groups[:, None]) & (request_ids[None, :] < request_ids[:, None])
    return lax.optimization_barrier(jnp.sum(earlier.astype(jnp.int32), axis=1))

def dequantize(values, scales):
    full_shape = values.shape
    widened = values.astype(jnp.float32).reshape(full_shape[:-1] + (scales.shape[-1], full_shape[-1] // scales.shape[-1]))
    return (widened * scales.astype(jnp.float32)[..., None]).reshape(full_shape).astype(jnp.bfloat16)

def attend(asked_rows, key_rows, value_rows, lengths, fresh_key, fresh_value):
    rows_count, span_len, width_all = key_rows.shape
    heads_kv = width_all // HD
    factor = 1.0 / math.sqrt(HD)
    grouped = asked_rows.astype(jnp.float32).reshape(rows_count, heads_kv, -1, HD)
    keyed = key_rows.astype(jnp.float32).reshape(rows_count, span_len, heads_kv, HD)
    valued = value_rows.astype(jnp.float32).reshape(rows_count, span_len, heads_kv, HD)
    usable = jnp.arange(span_len, dtype=jnp.int32)[None, :] < lengths[:, None]
    scores = jnp.einsum('rgjd,rlgd->rgjl', grouped, keyed, precision=HIGHEST) * factor
    scores = jnp.where(usable[:, None, None, :], scores, NEG_FILL)
    own_key = fresh_key.astype(jnp.float32).reshape(rows_count, heads_kv, HD)
    own_score = jnp.einsum('rgjd,rgd->rgj', grouped, own_key, precision=HIGHEST) * factor
    peak = jnp.maximum(lax.optimization_barrier(jnp.max(scores, axis=-1)), own_score)
    weights = jnp.where(usable[:, None, None, :], jnp.exp(scores - peak[..., None]), 0.0)
    own_weight = jnp.exp(own_score - peak)
    total = lax.optimization_barrier(jnp.sum(weights, axis=-1)) + own_weight
    rounded = lax.optimization_barrier(weights.astype(jnp.bfloat16)).astype(jnp.float32)
    own_rounded = lax.optimization_barrier(own_weight.astype(jnp.bfloat16)).astype(jnp.float32)
    summed = jnp.einsum('rgjl,rlgd->rgjd', rounded, valued, precision=HIGHEST)
    own_value = fresh_value.astype(jnp.float32).reshape(rows_count, heads_kv, 1, HD)
    summed = summed + own_rounded[..., None] * own_value
    return (summed / total[..., None]).reshape(rows_count, -1).astype(jnp.bfloat16)

def reference(queries, cache_kv, fresh_kv, ctx_len, prefill, prefill_scale, new_group, new_pages):
    ranking = group_ranks(new_group)
    slot_ids = new_group * NEW_GRP + ranking
    arrival = jnp.zeros((NEW,), jnp.int32).at[slot_ids].set(jnp.arange(NEW, dtype=jnp.int32))
    new_len = new_pages * PAGE
    handed = dequantize(prefill, prefill_scale)
    usable = jnp.arange(PROMPT, dtype=jnp.int32)[None, :] < new_len[:, None]
    handed = jnp.where(usable[None, :, :, None], handed, jnp.zeros((), jnp.bfloat16))
    handed_kv = handed[:, arrival].reshape(2, N_WIDE, NEW_GRP, PROMPT, KVH * HD)
    slot_len = new_len[arrival].reshape(N_WIDE, NEW_GRP)
    resident_len = ctx_len.reshape(N_WIDE, ROWS_GRP)
    resident = cache_kv.reshape(2, N_WIDE, ROWS_GRP, CTX, KVH * HD)

    def one_group(group_id):
        asked_rows = queries[group_id]
        own_fresh = fresh_kv[:, group_id]
        older_rows = attend(asked_rows[:ROWS_GRP], resident[0, group_id], resident[1, group_id], resident_len[group_id], own_fresh[0, :ROWS_GRP], own_fresh[1, :ROWS_GRP])
        newer_rows = attend(asked_rows[ROWS_GRP:], handed_kv[0, group_id], handed_kv[1, group_id], slot_len[group_id], own_fresh[0, ROWS_GRP:], own_fresh[1, ROWS_GRP:])
        return jnp.concatenate([older_rows, newer_rows], axis=0)
    attended = lax.map(one_group, jnp.arange(N_WIDE, dtype=jnp.int32))
    return (attended, handed_kv)
```

```python
import functools
import math

import jax
import jax.numpy as jnp
from jax import lax
from jax.experimental import pallas as pl
from jax.experimental.pallas import tpu as pltpu
from jax.sharding import PartitionSpec as P

HD = 128
PAGE = 16


NEG_FILL = -1e30


def group_ranks(groups):
    request_ids = jnp.arange(groups.shape[0], dtype=jnp.int32)
    earlier = (groups[None, :] == groups[:, None]) & (request_ids[None, :] < request_ids[:, None])
    return jnp.sum(earlier.astype(jnp.int32), axis=1)


def dequantize(values, scales):
    full_shape = values.shape
    widened = values.astype(jnp.float32).reshape(
        full_shape[:-1] + (scales.shape[-1], full_shape[-1] // scales.shape[-1])
    )
    return (
        (widened * scales.astype(jnp.float32)[..., None]).reshape(full_shape).astype(jnp.bfloat16)
    )


def self_score(asked_rows, fresh_key):
    rows_count = asked_rows.shape[0]
    heads_kv = fresh_key.shape[-1] // HD
    grouped = asked_rows.reshape(rows_count, heads_kv, -1, HD)
    own_key = fresh_key.reshape(rows_count, heads_kv, HD)
    return jnp.einsum("rgjd,rgd->rgj", grouped, own_key, preferred_element_type=jnp.float32) * (
        1.0 / math.sqrt(HD)
    )


def masked_scores(asked_rows, key_rows, usable):
    rows_count, span_len, width_all = key_rows.shape
    heads_kv = width_all // HD
    grouped = asked_rows.reshape(rows_count, heads_kv, -1, HD)
    keyed = key_rows.reshape(rows_count, span_len, heads_kv, HD)
    scores = jnp.einsum("rgjd,rlgd->rgjl", grouped, keyed, preferred_element_type=jnp.float32) * (
        1.0 / math.sqrt(HD)
    )
    return jnp.where(usable[:, None, None, :], scores, NEG_FILL)


def weighted_sum(weights, value_rows):
    rows_count, span_len, width_all = value_rows.shape
    valued = value_rows.reshape(rows_count, span_len, width_all // HD, HD)
    return jnp.einsum(
        "rgjl,rlgd->rgjd", weights.astype(jnp.bfloat16), valued, preferred_element_type=jnp.float32
    )


def own_term(own_weight, fresh_value):
    rows_count = fresh_value.shape[0]
    own_rounded = lax.optimization_barrier(own_weight.astype(jnp.bfloat16)).astype(jnp.float32)
    own_value = fresh_value.astype(jnp.float32).reshape(
        rows_count, fresh_value.shape[-1] // HD, 1, HD
    )
    return own_rounded[..., None] * own_value


def attend(asked_rows, key_rows, value_rows, lengths, fresh_key, fresh_value):
    rows_count = asked_rows.shape[0]
    usable = jnp.arange(key_rows.shape[1], dtype=jnp.int32)[None, :] < lengths[:, None]
    scores = masked_scores(asked_rows, key_rows, usable)
    own_score = self_score(asked_rows, fresh_key)
    peak = jnp.maximum(jnp.max(scores, axis=-1), own_score)
    weights = jnp.where(usable[:, None, None, :], jnp.exp(scores - peak[..., None]), 0.0)
    own_weight = jnp.exp(own_score - peak)
    total = jnp.sum(weights, axis=-1) + own_weight
    summed = weighted_sum(weights, value_rows) + own_term(own_weight, fresh_value)
    return (summed / total[..., None]).reshape(rows_count, -1).astype(jnp.bfloat16)


import numpy as np

LANES = 128
DELAY = 4
SLOTS = 16
STEP_CHOICES = (128, 160, 192, 224)
SPLITS = (0.0, 0.25, 0.5)


def ring_position(index, n):
    odd = index % 2
    return (1 - odd) * (index // 2) + odd * (n - 1 - index // 2)


def ring_device(position, n):
    far = position // (n // 2)
    return (1 - far) * (2 * position) + far * (2 * (n - 1 - position) + 1)


def plan_routes(new_group, new_pages):
    n = new_group.shape[0]
    nodes = jnp.arange(n, dtype=jnp.int32)
    order = np.array([ring_device(p, n) for p in range(n)])
    groups = new_group[order]
    pages = new_pages[order]
    hops_forward = (ring_position(groups, n) - nodes) % n
    hops_backward = (n - hops_forward) % n
    count = len(SPLITS) ** n
    digits = (np.arange(count)[:, None] // len(SPLITS) ** np.arange(n)[None, :]) % len(SPLITS)
    eighths = jnp.asarray((np.array(SPLITS) * 8)[digits].astype(np.int32))
    longer = (pages[None, :] * eighths) // 8
    shorter = pages[None, :] - longer
    short_forward = hops_forward[None, :] <= n // 2
    moving = (hops_forward > 0)[None, :]
    forward = jnp.where(moving, jnp.where(short_forward, shorter, longer), 0)
    backward = jnp.where(moving, jnp.where(short_forward, longer, shorter), 0)
    crossed_forward = ((nodes[None, :] - nodes[:, None]) % n) < hops_forward[:, None]
    crossed_backward = ((nodes[:, None] - nodes[None, :]) % n) < hops_backward[:, None]
    load_forward = jnp.dot(
        forward.astype(jnp.float32), crossed_forward.astype(jnp.float32), precision="highest"
    )
    load_backward = jnp.dot(
        backward.astype(jnp.float32), crossed_backward.astype(jnp.float32), precision="highest"
    )
    ends_forward = load_forward + jnp.where(forward > 0, (hops_forward - 1) * DELAY, 0)
    ends_backward = load_backward + jnp.where(backward > 0, (hops_backward - 1) * DELAY, 0)
    needed = jnp.max(jnp.maximum(ends_forward, ends_backward), axis=1).astype(jnp.int32)
    best = jnp.argmin(needed)
    steps = needed[best]
    forward, backward = forward[best], backward[best]
    mirror = (-np.arange(n)) % n
    limits = jnp.stack([forward, backward[mirror]])
    hops = jnp.stack([hops_forward, hops_backward[mirror]])
    firsts = jnp.stack([jnp.zeros((n,), jnp.int32), forward[mirror]])
    table = jnp.stack([limits, hops, firsts])
    table = jnp.pad(jnp.tile(table, (1, 1, LANES // n)), ((0, 0), (0, 6), (0, 0)))
    return steps, table


def handoff_kernel(
    n, steps, local_ref, table_ref, prefill_ref, scale_ref, out_ref,
    own, held, staged, hist, found, found_smem, send_sem, recv_sem, copy_sem,
):
    index = lax.axis_index("wide")
    place = ring_position(index, n)
    targets = (
        ring_device((place + 1) % n, n),
        ring_device((place + n - 1) % n, n),
    )
    barrier = pltpu.get_barrier_semaphore()
    for target in targets:
        pl.semaphore_signal(
            barrier, inc=1, device_id={"wide": target}, device_id_type=pl.DeviceIdType.MESH
        )
    pl.semaphore_wait(barrier, 2)

    pages = own.shape[0]
    width = prefill_ref.shape[-1]
    heads = width // HD

    def widen(page, carry):
        rows = pl.ds(pl.multiple_of(page * PAGE, PAGE), PAGE)
        for c in range(2):
            scale = scale_ref[c, 0, rows, :].astype(jnp.float32)
            values = prefill_ref[c, 0, rows, :].astype(jnp.float32)
            for h in range(heads):
                own[page, c, :, h * HD : (h + 1) * HD] = (
                    values[:, h * HD : (h + 1) * HD] * scale[:, h : h + 1]
                ).astype(jnp.bfloat16)
        return carry

    lax.fori_loop(0, pages, widen, 0)

    sublane = lax.broadcasted_iota(jnp.int32, (8, LANES), 0)
    lane = lax.broadcasted_iota(jnp.int32, (8, LANES), 1)
    mirrored = (n - place) % n
    here = ((sublane == 0) & (lane == place)) | ((sublane == 1) & (lane == mirrored))
    limits = table_ref[0]
    hops = table_ref[1]
    firsts = table_ref[2]

    def arrivals(step, seen, to_go, page):
        landed = jnp.where(here & (to_go == 1), page + 1, 0)
        landed = jnp.sum(landed, axis=1, keepdims=True)
        return jnp.where(lane == landed - 1, step - DELAY, seen)

    def advance(step, sent, seen, first):
        if first:
            to_go = jnp.zeros((8, LANES), jnp.int32)
            page = to_go
        else:
            past = hist[step % DELAY]
            past = pltpu.roll(past, 1, 1)
            to_go = past % 16
            page = past // 16
            seen = arrivals(step, seen, to_go, page)
        forwards = to_go > 1
        injects = jnp.logical_not(forwards) & (sent < limits)
        now = jnp.where(forwards, page * 16 + to_go - 1, jnp.where(injects, (firsts + sent) * 16 + hops, 0))
        hist[step % DELAY] = now
        code = jnp.where(here, jnp.where(forwards, pages, jnp.where(injects, firsts + sent, 0)), 0)
        codes = (
            jnp.sum(jnp.where(sublane == 0, code, 0)),
            jnp.sum(jnp.where(sublane == 1, code, 0)),
        )
        return sent + injects.astype(jnp.int32), seen, codes

    def hop(step, way):
        return pltpu.make_async_remote_copy(
            src_ref=staged.at[way, step % SLOTS],
            dst_ref=held.at[way, step],
            send_sem=send_sem.at[way, step % SLOTS],
            recv_sem=recv_sem.at[way, step % SLOTS],
            device_id={"wide": targets[way]},
            device_id_type=pl.DeviceIdType.MESH,
        )

    def one_step(step, carry, first, reuse):
        sent, seen = carry
        sent, seen, codes = advance(step, sent, seen, first)
        for way in range(2):
            if reuse:
                hop(step - SLOTS, way).wait_send()
            mine = own[jnp.minimum(codes[way], pages - 1)]
            if not first:
                hop(step - DELAY, way).wait_recv()
                mine = jnp.where(codes[way] >= pages, held[way, step - DELAY], mine)
            staged[way, step % SLOTS] = mine
            hop(step, way).start()
        return sent, seen

    carry = (jnp.zeros((8, LANES), jnp.int32), jnp.full((8, LANES), -1, jnp.int32))
    carry = lax.fori_loop(0, DELAY, lambda t, c: one_step(t, c, True, False), carry)
    carry = lax.fori_loop(DELAY, SLOTS, lambda t, c: one_step(t, c, False, False), carry)
    carry = lax.fori_loop(SLOTS, steps, lambda t, c: one_step(t, c, False, True), carry)
    sent, seen = carry

    def settle(step, seen):
        past = pltpu.roll(hist[step % DELAY], 1, 1)
        for way in range(2):
            hop(step - DELAY, way).wait_recv()
        return arrivals(step, seen, past % 16, past // 16)

    seen = lax.fori_loop(steps, steps + DELAY, settle, seen)

    def drain(step, carry):
        for way in range(2):
            hop(step, way).wait_send()
        return carry

    lax.fori_loop(steps - SLOTS, steps, drain, 0)

    found[...] = seen
    fetch = pltpu.make_async_copy(found, found_smem, copy_sem)
    fetch.start()
    fetch.wait()

    stays = local_ref[0]
    length = local_ref[1]

    def place_page(page, carry):
        forward = found_smem[0, page]
        backward = found_smem[1, page]
        from_backward = (backward >= 0).astype(jnp.int32)
        at = jnp.where(from_backward == 1, backward, jnp.maximum(forward, 0))
        rows = pl.ds(pl.multiple_of(page * PAGE, PAGE), PAGE)
        block = jnp.where(stays == 1, own[page], held[from_backward, at])
        block = jnp.where(page < length, block, jnp.zeros_like(block))
        for c in range(2):
            out_ref[c, 0, 0, rows, :] = block[c]
        return carry

    lax.fori_loop(0, pages, place_page, 0)


def handoff(steps, collective_id, n, local, table, prefill, prefill_scale):
    prompt_len, width = prefill.shape[2:]
    pages = prompt_len // PAGE
    return pl.pallas_call(
        functools.partial(handoff_kernel, n, steps),
        out_shape=jax.ShapeDtypeStruct((2, 1, 1, prompt_len, width), jnp.bfloat16),
        in_specs=[pl.BlockSpec(memory_space=pltpu.SMEM)]
        + [pl.BlockSpec(memory_space=pltpu.VMEM)] * 3,
        out_specs=pl.BlockSpec(memory_space=pltpu.VMEM),
        scratch_shapes=[
            pltpu.VMEM((pages, 2, PAGE, width), jnp.bfloat16),
            pltpu.VMEM((2, steps, 2, PAGE, width), jnp.bfloat16),
            pltpu.VMEM((2, SLOTS, 2, PAGE, width), jnp.bfloat16),
            pltpu.VMEM((DELAY, 8, LANES), jnp.int32),
            pltpu.VMEM((8, LANES), jnp.int32),
            pltpu.SMEM((8, LANES), jnp.int32),
            pltpu.SemaphoreType.DMA((2, SLOTS)),
            pltpu.SemaphoreType.DMA((2, SLOTS)),
            pltpu.SemaphoreType.DMA,
        ],
        compiler_params=pltpu.CompilerParams(
            collective_id=collective_id, has_side_effects=True, vmem_limit_bytes=50 * 2**20
        ),
    )(local, table, prefill, prefill_scale)


def exchange(prefill, prefill_scale, own_len, arrival, groups_count, per_group):
    prompt_len, width_here = prefill.shape[2:]
    positions = jnp.arange(prompt_len, dtype=jnp.int32)
    local_kv = dequantize(prefill, prefill_scale)
    keeping = positions[None, :] < own_len[:, None]
    local_kv = jnp.where(keeping[None, :, :, None], local_kv, jnp.zeros((), jnp.bfloat16))
    split_kv = local_kv.reshape(2, per_group, groups_count, prompt_len // groups_count, width_here)
    held = lax.all_to_all(split_kv, "wide", split_axis=2, concat_axis=1, tiled=True)
    ordered = held[:, arrival]
    return lax.all_to_all(ordered, "wide", split_axis=1, concat_axis=3, tiled=True)


def on_device(queries, cache_kv, fresh_kv, ctx_len, prefill, prefill_scale, new_group, new_pages):
    groups_count = lax.axis_size("wide")
    device_index = lax.axis_index("wide")
    new_total = new_group.shape[0]
    per_group = new_total // groups_count
    resident_count = cache_kv.shape[1]
    prompt_len = prefill.shape[2]
    slot_ids = new_group * per_group + group_ranks(new_group)
    arrival = (
        jnp.zeros((new_total,), jnp.int32).at[slot_ids].set(jnp.arange(new_total, dtype=jnp.int32))
    )
    new_len = new_pages * PAGE
    first_slot = device_index * per_group
    slot_len = lax.dynamic_slice_in_dim(new_len[arrival], first_slot, per_group)
    own_len = lax.dynamic_slice_in_dim(new_len, first_slot, per_group)
    asked_rows = queries[0]
    own_fresh = fresh_kv[:, 0]
    older_rows = attend(
        asked_rows[:resident_count],
        cache_kv[0],
        cache_kv[1],
        ctx_len,
        own_fresh[0, :resident_count],
        own_fresh[1, :resident_count],
    )

    def by_pieces():
        return exchange(prefill, prefill_scale, own_len, arrival, groups_count, per_group)

    if groups_count == 8 and per_group == 1 and prompt_len == LANES * PAGE:
        steps, table = plan_routes(new_group, new_pages)
        parts_count = lax.axis_size("parts")
        for shift in range(1, parts_count):
            steps = jnp.maximum(
                steps,
                lax.ppermute(
                    steps, "parts", [(p, (p + shift) % parts_count) for p in range(parts_count)]
                ),
            )
        source = lax.dynamic_index_in_dim(arrival, device_index, keepdims=False)
        local = jnp.stack([(source == device_index).astype(jnp.int32), slot_len[0] // PAGE])
        choice = sum((steps > limit).astype(jnp.int32) for limit in STEP_CHOICES)
        branches = [
            functools.partial(handoff, limit, 1 + i, groups_count, local, table, prefill, prefill_scale)
            for i, limit in enumerate(STEP_CHOICES)
        ]
        handed = lax.switch(choice, branches + [by_pieces])
    else:
        handed = by_pieces()
    newer_rows = attend(
        asked_rows[resident_count:],
        handed[0, 0],
        handed[1, 0],
        slot_len,
        own_fresh[0, resident_count:],
        own_fresh[1, resident_count:],
    )
    attended = jnp.concatenate([older_rows, newer_rows], axis=0)[None]
    return (attended, handed)


def solution(mesh):
    return jax.shard_map(
        on_device,
        mesh=mesh,
        in_specs=(
            P(("parts", "wide"), None, "tp"),
            P(None, ("parts", "wide"), None, "tp"),
            P(None, ("parts", "wide"), None, "tp"),
            P(("parts", "wide")),
            P(None, ("parts", "wide"), None, "tp"),
            P(None, ("parts", "wide"), None, "tp"),
            P("parts"),
            P("parts"),
        ),
        out_specs=(P(("parts", "wide"), None, "tp"), P(None, ("parts", "wide"), None, None, "tp")),
        check_vma=False,
    )
```

```python
import functools
import math

import jax
import jax.numpy as jnp
from jax import lax
from jax.experimental import pallas as pl
from jax.experimental.pallas import tpu as pltpu
from jax.sharding import PartitionSpec as P

HD = 128
PAGE = 16


NEG_FILL = -1e30


def group_ranks(groups):
    request_ids = jnp.arange(groups.shape[0], dtype=jnp.int32)
    earlier = (groups[None, :] == groups[:, None]) & (request_ids[None, :] < request_ids[:, None])
    return jnp.sum(earlier.astype(jnp.int32), axis=1)


def dequantize(values, scales):
    full_shape = values.shape
    widened = values.astype(jnp.float32).reshape(
        full_shape[:-1] + (scales.shape[-1], full_shape[-1] // scales.shape[-1])
    )
    return (
        (widened * scales.astype(jnp.float32)[..., None]).reshape(full_shape).astype(jnp.bfloat16)
    )


LANES = 128
DELAY = 4
SLOTS = 16
STEP_CHOICES = (112, 128, 144, 160, 176, 192, 208)


def ring_position(index, n):
    odd = index % 2
    return (1 - odd) * (index // 2) + odd * (n - 1 - index // 2)


def ring_device(position, n):
    far = position // (n // 2)
    return (1 - far) * (2 * position) + far * (2 * (n - 1 - position) + 1)


def plan_kernel(n, group_ref, pages_ref, index_ref, steps_ref, local_ref, table_ref):
    me = index_ref[0]
    order = [ring_device(p, n) for p in range(n)]
    pages = [pages_ref[d] for d in order]
    hops_forward = [(ring_position(group_ref[d], n) - p + n) % n for p, d in enumerate(order)]
    hops_backward = [(n - hops) % n for hops in hops_forward]
    count = 3**n
    rows = -(-count // (8 * LANES)) * 8
    number = lax.broadcasted_iota(jnp.int32, (rows, LANES), 0) * LANES + lax.broadcasted_iota(
        jnp.int32, (rows, LANES), 1
    )
    rest = number
    forward, backward = [], []

    def shares(digit, p):
        longer = (pages[p] * digit) // 4
        shorter = pages[p] - longer
        moving = (hops_forward[p] > 0).astype(jnp.int32)
        near = (hops_forward[p] <= n // 2).astype(jnp.int32)
        ahead = moving * (near * shorter + (1 - near) * longer)
        return ahead, moving * pages[p] - ahead

    for p in range(n):
        third = (rest * 43691) >> 17
        digit = rest - 3 * third
        rest = third
        ahead, back = shares(digit, p)
        forward.append(ahead)
        backward.append(back)
    needed = jnp.zeros((rows, LANES), jnp.int32)
    for e in range(n):
        for sent, hops, way in ((forward, hops_forward, 1), (backward, hops_backward, -1)):
            load = jnp.where(sent[e] > 0, jnp.maximum(hops[e] - 1, 0) * DELAY, 0)
            for p in range(n):
                load = load + sent[p] * (((e - p) * way % n) < hops[p]).astype(jnp.int32)
            needed = jnp.maximum(needed, load)
    span = rows * LANES
    key = jnp.min((needed * span + number).astype(jnp.float32)).astype(jnp.int32)
    steps_ref[0] = key // span
    best = key % span
    sublane = lax.broadcasted_iota(jnp.int32, (8, LANES), 0)
    lane = lax.broadcasted_iota(jnp.int32, (8, LANES), 1)
    limits = jnp.zeros((8, LANES), jnp.int32)
    hops = limits
    firsts = limits
    for p in range(n):
        ahead, back = shares(best % 3, p)
        best = best // 3
        here = (sublane == 0) & (lane % n == p)
        there = (sublane == 1) & (lane % n == (n - p) % n)
        limits = jnp.where(here, ahead, jnp.where(there, back, limits))
        hops = jnp.where(here, hops_forward[p], jnp.where(there, hops_backward[p], hops))
        firsts = jnp.where(there, ahead, firsts)
    table_ref[0] = limits
    table_ref[1] = hops
    table_ref[2] = firsts
    local_ref[0] = (group_ref[me] == me).astype(jnp.int32)
    local_ref[1] = sum(
        (group_ref[d] == me).astype(jnp.int32) * pages_ref[d] for d in range(n)
    )


def plan_routes(n, new_group, new_pages, device_index):
    return pl.pallas_call(
        functools.partial(plan_kernel, n),
        out_shape=(
            jax.ShapeDtypeStruct((1,), jnp.int32),
            jax.ShapeDtypeStruct((2,), jnp.int32),
            jax.ShapeDtypeStruct((3, 8, LANES), jnp.int32),
        ),
        in_specs=[pl.BlockSpec(memory_space=pltpu.SMEM)] * 3,
        out_specs=(
            pl.BlockSpec(memory_space=pltpu.SMEM),
            pl.BlockSpec(memory_space=pltpu.SMEM),
            pl.BlockSpec(memory_space=pltpu.VMEM),
        ),
    )(new_group, new_pages, device_index.reshape(1))


def attend_head(asked, own_key, own_value, keys, values, length):
    width = asked.shape[-1]
    grouped = jnp.concatenate([asked[:, at : at + HD] for at in range(0, width, HD)], axis=0)
    factor = 1.0 / math.sqrt(HD)
    scores = factor * lax.dot_general(
        grouped, keys, (((1,), (1,)), ((), ())), preferred_element_type=jnp.float32
    )
    usable = lax.broadcasted_iota(jnp.int32, scores.shape, 1) < length
    scores = jnp.where(usable, scores, NEG_FILL)
    own_score = factor * jnp.sum(
        grouped.astype(jnp.float32) * own_key.astype(jnp.float32), axis=1, keepdims=True
    )
    peak = jnp.maximum(jnp.max(scores, axis=1, keepdims=True), own_score)
    weights = jnp.where(usable, jnp.exp(scores - peak), 0.0)
    own_weight = jnp.exp(own_score - peak)
    total = jnp.sum(weights, axis=1, keepdims=True) + own_weight
    summed = jnp.dot(weights.astype(jnp.bfloat16), values, preferred_element_type=jnp.float32)
    own_rounded = own_weight.astype(jnp.bfloat16).astype(jnp.float32)
    summed = summed + own_rounded * own_value.astype(jnp.float32)
    result = (summed / total).astype(jnp.bfloat16)
    return jnp.concatenate([result[j : j + 1] for j in range(width // HD)], axis=1)


def older_kernel(length_ref, asked_ref, fresh_ref, cache_ref, out_ref):
    for r in range(out_ref.shape[0]):
        out_ref[r : r + 1, :] = attend_head(
            asked_ref[0, r : r + 1, :],
            fresh_ref[0, 0, r : r + 1, :],
            fresh_ref[1, 0, r : r + 1, :],
            cache_ref[0, r],
            cache_ref[1, r],
            length_ref[r],
        )


def older_attention(ctx_len, queries, fresh_kv, cache_kv):
    slots, width_asked = queries.shape[1:]
    resident_count, span_len, width = cache_kv.shape[1:]
    heads = width // HD
    asked = width_asked // heads
    return pl.pallas_call(
        older_kernel,
        grid=(heads,),
        out_shape=jax.ShapeDtypeStruct((resident_count, width_asked), jnp.bfloat16),
        in_specs=[
            pl.BlockSpec(memory_space=pltpu.SMEM),
            pl.BlockSpec((1, slots, asked), lambda h: (0, 0, h)),
            pl.BlockSpec((2, 1, slots, HD), lambda h: (0, 0, 0, h)),
            pl.BlockSpec((2, resident_count, span_len, HD), lambda h: (0, 0, 0, h)),
        ],
        out_specs=pl.BlockSpec((resident_count, asked), lambda h: (0, h)),
        compiler_params=pltpu.CompilerParams(vmem_limit_bytes=24 * 2**20),
    )(ctx_len, queries, fresh_kv, cache_kv)


def newer_kernel(length_ref, asked_ref, fresh_ref, older_ref, handed_ref, out_ref, kept_ref):
    kept_ref[...] = handed_ref[...]
    older = older_ref.shape[0]
    out_ref[0, :older, :] = older_ref[...]
    for r in range(handed_ref.shape[2]):
        out_ref[0, older + r : older + r + 1, :] = attend_head(
            asked_ref[0, older + r : older + r + 1, :],
            fresh_ref[0, 0, older + r : older + r + 1, :],
            fresh_ref[1, 0, older + r : older + r + 1, :],
            handed_ref[0, 0, r],
            handed_ref[1, 0, r],
            length_ref[r],
        )


def newer_attention(slot_len, queries, fresh_kv, older_rows, handed):
    slots, width_asked = queries.shape[1:]
    per_group, prompt_len, width = handed.shape[2:]
    heads = width // HD
    asked = width_asked // heads
    asked_spec = pl.BlockSpec((1, slots, asked), lambda h: (0, 0, h))
    handed_spec = pl.BlockSpec((2, 1, per_group, prompt_len, HD), lambda h: (0, 0, 0, 0, h))
    return pl.pallas_call(
        newer_kernel,
        grid=(heads,),
        out_shape=(
            jax.ShapeDtypeStruct(queries.shape, jnp.bfloat16),
            jax.ShapeDtypeStruct(handed.shape, jnp.bfloat16),
        ),
        in_specs=[
            pl.BlockSpec(memory_space=pltpu.SMEM),
            asked_spec,
            pl.BlockSpec((2, 1, slots, HD), lambda h: (0, 0, 0, h)),
            pl.BlockSpec((older_rows.shape[0], asked), lambda h: (0, h)),
            handed_spec,
        ],
        out_specs=(asked_spec, handed_spec),
        compiler_params=pltpu.CompilerParams(vmem_limit_bytes=24 * 2**20),
    )(slot_len, queries, fresh_kv, older_rows, handed)


def handoff_kernel(
    n, steps, local_ref, table_ref, prefill_ref, scale_ref, out_ref,
    held, staged, hist, found, found_smem, send_sem, recv_sem, copy_sem,
):
    index = lax.axis_index("wide")
    place = ring_position(index, n)
    targets = (
        ring_device((place + 1) % n, n),
        ring_device((place + n - 1) % n, n),
    )
    barrier = pltpu.get_barrier_semaphore()
    for target in targets:
        pl.semaphore_signal(
            barrier, inc=1, device_id={"wide": target}, device_id_type=pl.DeviceIdType.MESH
        )
    pl.semaphore_wait(barrier, 2)

    pages = prefill_ref.shape[1]
    width = prefill_ref.shape[-1]
    heads = width // HD

    def widen(page):
        blocks = []
        for c in range(2):
            scale = scale_ref[c, page].astype(jnp.float32)
            values = prefill_ref[c, page].astype(jnp.float32)
            columns = [
                values[:, h * HD : (h + 1) * HD] * scale[:, h : h + 1] for h in range(heads)
            ]
            blocks.append(jnp.concatenate(columns, axis=1).astype(jnp.bfloat16))
        return blocks

    def keep_page(page):
        rows = pl.ds(pl.multiple_of(page * PAGE, PAGE), PAGE)
        for c, block in enumerate(widen(page)):
            out_ref[c, 0, 0, rows, :] = block

    sublane = lax.broadcasted_iota(jnp.int32, (8, LANES), 0)
    lane = lax.broadcasted_iota(jnp.int32, (8, LANES), 1)
    mirrored = (n - place) % n
    here = ((sublane == 0) & (lane == place)) | ((sublane == 1) & (lane == mirrored))
    limits = table_ref[0]
    hops = table_ref[1]
    firsts = table_ref[2]

    def arrivals(step, seen, to_go, page):
        landed = jnp.where(here & (to_go == 1), page + 1, 0)
        landed = jnp.sum(landed, axis=1, keepdims=True)
        return jnp.where(lane == landed - 1, step - DELAY, seen)

    def advance(step, sent, seen, first):
        if first:
            to_go = jnp.zeros((8, LANES), jnp.int32)
            page = to_go
        else:
            past = hist[step % DELAY]
            past = pltpu.roll(past, 1, 1)
            to_go = past % 16
            page = past // 16
            seen = arrivals(step, seen, to_go, page)
        forwards = to_go > 1
        injects = jnp.logical_not(forwards) & (sent < limits)
        now = jnp.where(forwards, page * 16 + to_go - 1, jnp.where(injects, (firsts + sent) * 16 + hops, 0))
        hist[step % DELAY] = now
        code = jnp.where(here, jnp.where(forwards, pages, jnp.where(injects, firsts + sent, 0)), 0)
        codes = (
            jnp.sum(jnp.where(sublane == 0, code, 0)),
            jnp.sum(jnp.where(sublane == 1, code, 0)),
        )
        return sent + injects.astype(jnp.int32), seen, codes

    def hop(step, way):
        return pltpu.make_async_remote_copy(
            src_ref=staged.at[way, step % SLOTS],
            dst_ref=held.at[way, step],
            send_sem=send_sem.at[way, step % SLOTS],
            recv_sem=recv_sem.at[way, step % SLOTS],
            device_id={"wide": targets[way]},
            device_id_type=pl.DeviceIdType.MESH,
        )

    def one_step(step, carry, first, reuse):
        sent, seen = carry
        sent, seen, codes = advance(step, sent, seen, first)
        for way in range(2):
            if reuse:
                hop(step - SLOTS, way).wait_send()
            mine = widen(jnp.minimum(codes[way], pages - 1))
            if not first:
                hop(step - DELAY, way).wait_recv()
            for c in range(2):
                block = mine[c]
                if not first:
                    block = jnp.where(codes[way] >= pages, held[way, step - DELAY, c], block)
                staged[way, step % SLOTS, c] = block
            hop(step, way).start()
        keep_page(step % pages)
        return sent, seen

    carry = (jnp.zeros((8, LANES), jnp.int32), jnp.full((8, LANES), -1, jnp.int32))
    carry = lax.fori_loop(0, DELAY, lambda t, c: one_step(t, c, True, False), carry)
    carry = lax.fori_loop(DELAY, SLOTS, lambda t, c: one_step(t, c, False, False), carry)
    carry = lax.fori_loop(SLOTS, steps, lambda t, c: one_step(t, c, False, True), carry)
    sent, seen = carry

    def keep_late(page, carry):
        keep_page(page)
        return carry

    lax.fori_loop(min(steps, pages), pages, keep_late, 0)

    def settle(step, seen):
        past = pltpu.roll(hist[step % DELAY], 1, 1)
        for way in range(2):
            hop(step - DELAY, way).wait_recv()
        return arrivals(step, seen, past % 16, past // 16)

    seen = lax.fori_loop(steps, steps + DELAY, settle, seen)

    def drain(step, carry):
        for way in range(2):
            hop(step, way).wait_send()
        return carry

    lax.fori_loop(steps - SLOTS, steps, drain, 0)

    found[...] = seen
    fetch = pltpu.make_async_copy(found, found_smem, copy_sem)
    fetch.start()
    fetch.wait()

    stays = local_ref[0]
    length = local_ref[1]

    def place_page(page, carry):
        forward = found_smem[0, page]
        backward = found_smem[1, page]
        from_backward = (backward >= 0).astype(jnp.int32)
        at = jnp.where(from_backward == 1, backward, jnp.maximum(forward, 0))
        rows = pl.ds(pl.multiple_of(page * PAGE, PAGE), PAGE)
        for c in range(2):
            block = jnp.where(stays == 1, out_ref[c, 0, 0, rows, :], held[from_backward, at, c])
            out_ref[c, 0, 0, rows, :] = jnp.where(page < length, block, jnp.zeros_like(block))
        return carry

    lax.fori_loop(0, pages, place_page, 0)


def handoff(steps, collective_id, n, local, table, prefill, prefill_scale):
    prompt_len, width = prefill.shape[2:]
    return pl.pallas_call(
        functools.partial(handoff_kernel, n, steps),
        out_shape=jax.ShapeDtypeStruct((2, 1, 1, prompt_len, width), jnp.bfloat16),
        in_specs=[pl.BlockSpec(memory_space=pltpu.SMEM)]
        + [pl.BlockSpec(memory_space=pltpu.VMEM)] * 3,
        out_specs=pl.BlockSpec(memory_space=pltpu.VMEM),
        scratch_shapes=[
            pltpu.VMEM((2, steps, 2, PAGE, width), jnp.bfloat16),
            pltpu.VMEM((2, SLOTS, 2, PAGE, width), jnp.bfloat16),
            pltpu.VMEM((DELAY, 8, LANES), jnp.int32),
            pltpu.VMEM((8, LANES), jnp.int32),
            pltpu.SMEM((8, LANES), jnp.int32),
            pltpu.SemaphoreType.DMA((2, SLOTS)),
            pltpu.SemaphoreType.DMA((2, SLOTS)),
            pltpu.SemaphoreType.DMA,
        ],
        compiler_params=pltpu.CompilerParams(
            collective_id=collective_id, has_side_effects=True, vmem_limit_bytes=50 * 2**20
        ),
    )(
        local,
        table,
        prefill.reshape(2, -1, PAGE, width),
        prefill_scale.reshape(2, -1, PAGE, width // HD),
    )


def exchange(prefill, prefill_scale, own_len, arrival, groups_count, per_group):
    prompt_len, width_here = prefill.shape[2:]
    positions = jnp.arange(prompt_len, dtype=jnp.int32)
    local_kv = dequantize(prefill, prefill_scale)
    keeping = positions[None, :] < own_len[:, None]
    local_kv = jnp.where(keeping[None, :, :, None], local_kv, jnp.zeros((), jnp.bfloat16))
    split_kv = local_kv.reshape(2, per_group, groups_count, prompt_len // groups_count, width_here)
    held = lax.all_to_all(split_kv, "wide", split_axis=2, concat_axis=1, tiled=True)
    ordered = held[:, arrival]
    return lax.all_to_all(ordered, "wide", split_axis=1, concat_axis=3, tiled=True)


def on_device(queries, cache_kv, fresh_kv, ctx_len, prefill, prefill_scale, new_group, new_pages):
    groups_count = lax.axis_size("wide")
    device_index = lax.axis_index("wide")
    new_total = new_group.shape[0]
    per_group = new_total // groups_count
    prompt_len = prefill.shape[2]
    slot_ids = new_group * per_group + group_ranks(new_group)
    arrival = (
        jnp.zeros((new_total,), jnp.int32).at[slot_ids].set(jnp.arange(new_total, dtype=jnp.int32))
    )
    new_len = new_pages * PAGE
    first_slot = device_index * per_group
    slot_len = lax.dynamic_slice_in_dim(new_len[arrival], first_slot, per_group)
    own_len = lax.dynamic_slice_in_dim(new_len, first_slot, per_group)
    def by_pieces():
        return exchange(prefill, prefill_scale, own_len, arrival, groups_count, per_group)

    if groups_count == 8 and per_group == 1 and prompt_len == LANES * PAGE:
        steps, local, table = plan_routes(groups_count, new_group, new_pages, device_index)
        parts_count = lax.axis_size("parts")
        most = steps
        for shift in range(1, parts_count):
            there = [(p, (p + shift) % parts_count) for p in range(parts_count)]
            most = jnp.maximum(most, lax.ppermute(steps, "parts", there))
        older_rows = older_attention(ctx_len, queries, fresh_kv, cache_kv)
        choice = sum((most[0] > limit).astype(jnp.int32) for limit in STEP_CHOICES)
        branches = [
            functools.partial(handoff, limit, 1 + i, groups_count, local, table, prefill, prefill_scale)
            for i, limit in enumerate(STEP_CHOICES)
        ]
        handed = lax.switch(choice, branches + [by_pieces])
    else:
        older_rows = older_attention(ctx_len, queries, fresh_kv, cache_kv)
        handed = by_pieces()
    return newer_attention(slot_len, queries, fresh_kv, older_rows, handed)


def solution(mesh):
    return jax.shard_map(
        on_device,
        mesh=mesh,
        in_specs=(
            P(("parts", "wide"), None, "tp"),
            P(None, ("parts", "wide"), None, "tp"),
            P(None, ("parts", "wide"), None, "tp"),
            P(("parts", "wide")),
            P(None, ("parts", "wide"), None, "tp"),
            P(None, ("parts", "wide"), None, "tp"),
            P("parts"),
            P("parts"),
        ),
        out_specs=(P(("parts", "wide"), None, "tp"), P(None, ("parts", "wide"), None, None, "tp")),
        check_vma=False,
    )
```

```python
import functools
import math

import jax
import jax.numpy as jnp
from jax import lax
from jax.experimental import pallas as pl
from jax.experimental.pallas import tpu as pltpu
from jax.sharding import PartitionSpec as P

HD = 128
PAGE = 16


NEG_FILL = -1e30


def group_ranks(groups):
    request_ids = jnp.arange(groups.shape[0], dtype=jnp.int32)
    earlier = (groups[None, :] == groups[:, None]) & (request_ids[None, :] < request_ids[:, None])
    return jnp.sum(earlier.astype(jnp.int32), axis=1)


def dequantize(values, scales):
    full_shape = values.shape
    widened = values.astype(jnp.float32).reshape(
        full_shape[:-1] + (scales.shape[-1], full_shape[-1] // scales.shape[-1])
    )
    return (
        (widened * scales.astype(jnp.float32)[..., None]).reshape(full_shape).astype(jnp.bfloat16)
    )


LANES = 128
DELAY = 5
SLOTS = 20
STEP_CHOICES = tuple(range(112, 208, 8))


def ring_position(index, n):
    odd = index % 2
    return (1 - odd) * (index // 2) + odd * (n - 1 - index // 2)


def ring_device(position, n):
    far = position // (n // 2)
    return (1 - far) * (2 * position) + far * (2 * (n - 1 - position) + 1)


def plan_kernel(n, group_ref, pages_ref, index_ref, steps_ref, local_ref, length_ref, table_ref):
    me = index_ref[0]
    order = [ring_device(p, n) for p in range(n)]
    pages = [pages_ref[d] for d in order]
    hops_forward = [(ring_position(group_ref[d], n) - p + n) % n for p, d in enumerate(order)]
    hops_backward = [(n - hops) % n for hops in hops_forward]
    count = 3**n
    rows = -(-count // (8 * LANES)) * 8
    number = lax.broadcasted_iota(jnp.int32, (rows, LANES), 0) * LANES + lax.broadcasted_iota(
        jnp.int32, (rows, LANES), 1
    )
    rest = number
    forward, backward = [], []

    def shares(digit, p):
        longer = (pages[p] * digit) // 4
        shorter = pages[p] - longer
        moving = (hops_forward[p] > 0).astype(jnp.int32)
        near = (hops_forward[p] <= n // 2).astype(jnp.int32)
        ahead = moving * (near * shorter + (1 - near) * longer)
        return ahead, moving * pages[p] - ahead

    for p in range(n):
        third = (rest * 43691) >> 17
        digit = rest - 3 * third
        rest = third
        ahead, back = shares(digit, p)
        forward.append(ahead)
        backward.append(back)
    needed = jnp.zeros((rows, LANES), jnp.int32)
    for e in range(n):
        for sent, hops, way in ((forward, hops_forward, 1), (backward, hops_backward, -1)):
            load = jnp.where(sent[e] > 0, jnp.maximum(hops[e] - 1, 0) * DELAY, 0)
            for p in range(n):
                load = load + sent[p] * (((e - p) * way % n) < hops[p]).astype(jnp.int32)
            needed = jnp.maximum(needed, load)
    span = rows * LANES
    key = jnp.min((needed * span + number).astype(jnp.float32)).astype(jnp.int32)
    steps_ref[0] = key // span
    best = key % span
    sublane = lax.broadcasted_iota(jnp.int32, (8, LANES), 0)
    lane = lax.broadcasted_iota(jnp.int32, (8, LANES), 1)
    limits = jnp.zeros((8, LANES), jnp.int32)
    hops = limits
    firsts = limits
    for p in range(n):
        ahead, back = shares(best % 3, p)
        best = best // 3
        here = (sublane == 0) & (lane % n == p)
        there = (sublane == 1) & (lane % n == (n - p) % n)
        limits = jnp.where(here, ahead, jnp.where(there, back, limits))
        hops = jnp.where(here, hops_forward[p], jnp.where(there, hops_backward[p], hops))
        firsts = jnp.where(there, ahead, firsts)
    table_ref[0] = limits
    table_ref[1] = hops
    table_ref[2] = firsts
    local_ref[0] = (group_ref[me] == me).astype(jnp.int32)
    length = sum((group_ref[d] == me).astype(jnp.int32) * pages_ref[d] for d in range(n))
    local_ref[1] = length
    length_ref[0] = length * PAGE


def plan_routes(n, new_group, new_pages, device_index):
    return pl.pallas_call(
        functools.partial(plan_kernel, n),
        out_shape=(
            jax.ShapeDtypeStruct((1,), jnp.int32),
            jax.ShapeDtypeStruct((2,), jnp.int32),
            jax.ShapeDtypeStruct((1,), jnp.int32),
            jax.ShapeDtypeStruct((3, 8, LANES), jnp.int32),
        ),
        in_specs=[pl.BlockSpec(memory_space=pltpu.SMEM)] * 3,
        out_specs=(
            pl.BlockSpec(memory_space=pltpu.SMEM),
            pl.BlockSpec(memory_space=pltpu.SMEM),
            pl.BlockSpec(memory_space=pltpu.SMEM),
            pl.BlockSpec(memory_space=pltpu.VMEM),
        ),
    )(new_group, new_pages, device_index.reshape(1))


def attend_head(asked, own_key, own_value, keys, values, length):
    width = asked.shape[-1]
    grouped = jnp.concatenate([asked[:, at : at + HD] for at in range(0, width, HD)], axis=0)
    factor = 1.0 / math.sqrt(HD)
    scores = factor * lax.dot_general(
        grouped, keys, (((1,), (1,)), ((), ())), preferred_element_type=jnp.float32
    )
    usable = lax.broadcasted_iota(jnp.int32, scores.shape, 1) < length
    scores = jnp.where(usable, scores, NEG_FILL)
    own_score = factor * jnp.sum(
        grouped.astype(jnp.float32) * own_key.astype(jnp.float32), axis=1, keepdims=True
    )
    peak = jnp.maximum(jnp.max(scores, axis=1, keepdims=True), own_score)
    weights = jnp.where(usable, jnp.exp(scores - peak), 0.0)
    own_weight = jnp.exp(own_score - peak)
    total = jnp.sum(weights, axis=1, keepdims=True) + own_weight
    summed = jnp.dot(weights.astype(jnp.bfloat16), values, preferred_element_type=jnp.float32)
    own_rounded = own_weight.astype(jnp.bfloat16).astype(jnp.float32)
    summed = summed + own_rounded * own_value.astype(jnp.float32)
    result = (summed / total).astype(jnp.bfloat16)
    return jnp.concatenate([result[j : j + 1] for j in range(width // HD)], axis=1)


def older_kernel(length_ref, asked_ref, fresh_ref, cache_ref, out_ref):
    for r in range(out_ref.shape[0]):
        out_ref[r : r + 1, :] = attend_head(
            asked_ref[0, r : r + 1, :],
            fresh_ref[0, 0, r : r + 1, :],
            fresh_ref[1, 0, r : r + 1, :],
            cache_ref[0, r],
            cache_ref[1, r],
            length_ref[r],
        )


def older_attention(ctx_len, queries, fresh_kv, cache_kv):
    slots, width_asked = queries.shape[1:]
    resident_count, span_len, width = cache_kv.shape[1:]
    heads = width // HD
    asked = width_asked // heads
    return pl.pallas_call(
        older_kernel,
        grid=(heads,),
        out_shape=jax.ShapeDtypeStruct((resident_count, width_asked), jnp.bfloat16),
        in_specs=[
            pl.BlockSpec(memory_space=pltpu.SMEM),
            pl.BlockSpec((1, slots, asked), lambda h: (0, 0, h)),
            pl.BlockSpec((2, 1, slots, HD), lambda h: (0, 0, 0, h)),
            pl.BlockSpec((2, resident_count, span_len, HD), lambda h: (0, 0, 0, h)),
        ],
        out_specs=pl.BlockSpec((resident_count, asked), lambda h: (0, h)),
        compiler_params=pltpu.CompilerParams(vmem_limit_bytes=24 * 2**20),
    )(ctx_len, queries, fresh_kv, cache_kv)


def newer_kernel(length_ref, asked_ref, fresh_ref, older_ref, handed_ref, out_ref, kept_ref):
    kept_ref[...] = handed_ref[...]
    older = older_ref.shape[0]
    out_ref[0, :older, :] = older_ref[...]
    for r in range(handed_ref.shape[2]):
        out_ref[0, older + r : older + r + 1, :] = attend_head(
            asked_ref[0, older + r : older + r + 1, :],
            fresh_ref[0, 0, older + r : older + r + 1, :],
            fresh_ref[1, 0, older + r : older + r + 1, :],
            handed_ref[0, 0, r],
            handed_ref[1, 0, r],
            length_ref[r],
        )


def newer_attention(slot_len, queries, fresh_kv, older_rows, handed):
    slots, width_asked = queries.shape[1:]
    per_group, prompt_len, width = handed.shape[2:]
    heads = width // HD
    asked = width_asked // heads
    asked_spec = pl.BlockSpec((1, slots, asked), lambda h: (0, 0, h))
    handed_spec = pl.BlockSpec((2, 1, per_group, prompt_len, HD), lambda h: (0, 0, 0, 0, h))
    return pl.pallas_call(
        newer_kernel,
        grid=(heads,),
        out_shape=(
            jax.ShapeDtypeStruct(queries.shape, jnp.bfloat16),
            jax.ShapeDtypeStruct(handed.shape, jnp.bfloat16),
        ),
        in_specs=[
            pl.BlockSpec(memory_space=pltpu.SMEM),
            asked_spec,
            pl.BlockSpec((2, 1, slots, HD), lambda h: (0, 0, 0, h)),
            pl.BlockSpec((older_rows.shape[0], asked), lambda h: (0, h)),
            handed_spec,
        ],
        out_specs=(asked_spec, handed_spec),
        compiler_params=pltpu.CompilerParams(vmem_limit_bytes=24 * 2**20),
    )(slot_len, queries, fresh_kv, older_rows, handed)


def handoff_kernel(
    n, steps, local_ref, table_ref, prefill_ref, scale_ref,
    length_ref, asked_ref, fresh_ref, cache_ref, older_ref, out_ref,
    held, staged, hist, found, found_smem, send_sem, recv_sem, copy_sem,
):
    index = lax.axis_index("wide")
    place = ring_position(index, n)
    targets = (
        ring_device((place + 1) % n, n),
        ring_device((place + n - 1) % n, n),
    )
    barrier = pltpu.get_barrier_semaphore()
    for target in targets:
        pl.semaphore_signal(
            barrier, inc=1, device_id={"wide": target}, device_id_type=pl.DeviceIdType.MESH
        )
    pl.semaphore_wait(barrier, 2)

    pages = prefill_ref.shape[1]
    width = prefill_ref.shape[-1]
    heads = width // HD

    def widen(page):
        blocks = []
        for c in range(2):
            scale = scale_ref[c, page].astype(jnp.float32)
            values = prefill_ref[c, page].astype(jnp.float32)
            columns = [
                values[:, h * HD : (h + 1) * HD] * scale[:, h : h + 1] for h in range(heads)
            ]
            blocks.append(jnp.concatenate(columns, axis=1).astype(jnp.bfloat16))
        return blocks

    def keep_page(page):
        rows = pl.ds(pl.multiple_of(page * PAGE, PAGE), PAGE)
        for c, block in enumerate(widen(page)):
            out_ref[c, 0, 0, rows, :] = block

    sublane = lax.broadcasted_iota(jnp.int32, (8, LANES), 0)
    lane = lax.broadcasted_iota(jnp.int32, (8, LANES), 1)
    mirrored = (n - place) % n
    here = ((sublane == 0) & (lane == place)) | ((sublane == 1) & (lane == mirrored))
    limits = table_ref[0]
    hops = table_ref[1]
    firsts = table_ref[2]

    def arrivals(step, seen, to_go, page):
        landed = jnp.where(here & (to_go == 1), page + 1, 0)
        landed = jnp.sum(landed, axis=1, keepdims=True)
        return jnp.where(lane == landed - 1, step - DELAY, seen)

    def advance(step, sent, seen, first):
        if first:
            to_go = jnp.zeros((8, LANES), jnp.int32)
            page = to_go
        else:
            past = hist[step % DELAY]
            past = pltpu.roll(past, 1, 1)
            to_go = past % 16
            page = past // 16
            seen = arrivals(step, seen, to_go, page)
        forwards = to_go > 1
        injects = jnp.logical_not(forwards) & (sent < limits)
        now = jnp.where(forwards, page * 16 + to_go - 1, jnp.where(injects, (firsts + sent) * 16 + hops, 0))
        hist[step % DELAY] = now
        code = jnp.where(here, jnp.where(forwards, pages, jnp.where(injects, firsts + sent, 0)), 0)
        codes = (
            jnp.sum(jnp.where(sublane == 0, code, 0)),
            jnp.sum(jnp.where(sublane == 1, code, 0)),
        )
        return sent + injects.astype(jnp.int32), seen, codes

    def hop(step, way):
        return pltpu.make_async_remote_copy(
            src_ref=staged.at[way, step % SLOTS],
            dst_ref=held.at[way, step],
            send_sem=send_sem.at[way, step % SLOTS],
            recv_sem=recv_sem.at[way, step % SLOTS],
            device_id={"wide": targets[way]},
            device_id_type=pl.DeviceIdType.MESH,
        )

    def one_step(step, carry, first, reuse):
        sent, seen = carry
        sent, seen, codes = advance(step, sent, seen, first)
        for way in range(2):
            if reuse:
                hop(step - SLOTS, way).wait_send()
            mine = widen(jnp.minimum(codes[way], pages - 1))
            if not first:
                hop(step - DELAY, way).wait_recv()
            for c in range(2):
                block = mine[c]
                if not first:
                    block = jnp.where(codes[way] >= pages, held[way, step - DELAY, c], block)
                staged[way, step % SLOTS, c] = block
            hop(step, way).start()
        keep_page(step % pages)
        return sent, seen

    carry = (jnp.zeros((8, LANES), jnp.int32), jnp.full((8, LANES), -1, jnp.int32))
    carry = lax.fori_loop(0, DELAY, lambda t, c: one_step(t, c, True, False), carry)
    carry = lax.fori_loop(DELAY, SLOTS, lambda t, c: one_step(t, c, False, False), carry)
    resident_count = cache_ref.shape[1]
    asked = asked_ref.shape[-1] // heads
    between = (steps - SLOTS) // (heads + 1)

    def attend_older(head):
        columns = pl.ds(pl.multiple_of(head * HD, HD), HD)
        outer = pl.ds(pl.multiple_of(head * asked, asked), asked)
        for r in range(resident_count):
            older_ref[r : r + 1, outer] = attend_head(
                asked_ref[0, r : r + 1, outer],
                fresh_ref[0, 0, r : r + 1, columns],
                fresh_ref[1, 0, r : r + 1, columns],
                cache_ref[0, r, :, columns],
                cache_ref[1, r, :, columns],
                length_ref[r],
            )

    def stretch(head, carry):
        start = SLOTS + head * between
        carry = lax.fori_loop(
            start, start + between, lambda t, c: one_step(t, c, False, True), carry
        )
        attend_older(head)
        return carry

    carry = lax.fori_loop(0, heads, stretch, carry)
    carry = lax.fori_loop(
        SLOTS + heads * between, steps, lambda t, c: one_step(t, c, False, True), carry
    )
    sent, seen = carry

    def keep_late(page, carry):
        keep_page(page)
        return carry

    lax.fori_loop(min(steps, pages), pages, keep_late, 0)

    def settle(step, seen):
        past = pltpu.roll(hist[step % DELAY], 1, 1)
        for way in range(2):
            hop(step - DELAY, way).wait_recv()
        return arrivals(step, seen, past % 16, past // 16)

    seen = lax.fori_loop(steps, steps + DELAY, settle, seen)

    def drain(step, carry):
        for way in range(2):
            hop(step, way).wait_send()
        return carry

    lax.fori_loop(steps - SLOTS, steps, drain, 0)

    found[...] = seen
    fetch = pltpu.make_async_copy(found, found_smem, copy_sem)
    fetch.start()
    fetch.wait()

    stays = local_ref[0]
    length = local_ref[1]

    def place_page(page, carry):
        forward = found_smem[0, page]
        backward = found_smem[1, page]
        from_backward = (backward >= 0).astype(jnp.int32)
        at = jnp.where(from_backward == 1, backward, jnp.maximum(forward, 0))
        rows = pl.ds(pl.multiple_of(page * PAGE, PAGE), PAGE)
        for c in range(2):
            block = jnp.where(stays == 1, out_ref[c, 0, 0, rows, :], held[from_backward, at, c])
            out_ref[c, 0, 0, rows, :] = jnp.where(page < length, block, jnp.zeros_like(block))
        return carry

    lax.fori_loop(0, pages, place_page, 0)


def handoff(
    steps, collective_id, n, local, table, prefill, prefill_scale,
    ctx_len, queries, fresh_kv, cache_kv,
):
    prompt_len, width = prefill.shape[2:]
    return pl.pallas_call(
        functools.partial(handoff_kernel, n, steps),
        out_shape=(
            jax.ShapeDtypeStruct((cache_kv.shape[1], queries.shape[2]), jnp.bfloat16),
            jax.ShapeDtypeStruct((2, 1, 1, prompt_len, width), jnp.bfloat16),
        ),
        in_specs=[pl.BlockSpec(memory_space=pltpu.SMEM)]
        + [pl.BlockSpec(memory_space=pltpu.VMEM)] * 3
        + [pl.BlockSpec(memory_space=pltpu.SMEM)]
        + [pl.BlockSpec(memory_space=pltpu.VMEM)] * 3,
        out_specs=(pl.BlockSpec(memory_space=pltpu.VMEM),) * 2,
        scratch_shapes=[
            pltpu.VMEM((2, steps, 2, PAGE, width), jnp.bfloat16),
            pltpu.VMEM((2, SLOTS, 2, PAGE, width), jnp.bfloat16),
            pltpu.VMEM((DELAY, 8, LANES), jnp.int32),
            pltpu.VMEM((8, LANES), jnp.int32),
            pltpu.SMEM((8, LANES), jnp.int32),
            pltpu.SemaphoreType.DMA((2, SLOTS)),
            pltpu.SemaphoreType.DMA((2, SLOTS)),
            pltpu.SemaphoreType.DMA,
        ],
        compiler_params=pltpu.CompilerParams(
            collective_id=collective_id, has_side_effects=True, vmem_limit_bytes=50 * 2**20
        ),
    )(
        local,
        table,
        prefill.reshape(2, -1, PAGE, width),
        prefill_scale.reshape(2, -1, PAGE, width // HD),
        ctx_len,
        queries,
        fresh_kv,
        cache_kv,
    )


def exchange(prefill, prefill_scale, own_len, arrival, groups_count, per_group):
    prompt_len, width_here = prefill.shape[2:]
    positions = jnp.arange(prompt_len, dtype=jnp.int32)
    local_kv = dequantize(prefill, prefill_scale)
    keeping = positions[None, :] < own_len[:, None]
    local_kv = jnp.where(keeping[None, :, :, None], local_kv, jnp.zeros((), jnp.bfloat16))
    split_kv = local_kv.reshape(2, per_group, groups_count, prompt_len // groups_count, width_here)
    held = lax.all_to_all(split_kv, "wide", split_axis=2, concat_axis=1, tiled=True)
    ordered = held[:, arrival]
    return lax.all_to_all(ordered, "wide", split_axis=1, concat_axis=3, tiled=True)


def on_device(queries, cache_kv, fresh_kv, ctx_len, prefill, prefill_scale, new_group, new_pages):
    groups_count = lax.axis_size("wide")
    device_index = lax.axis_index("wide")
    new_total = new_group.shape[0]
    per_group = new_total // groups_count
    prompt_len = prefill.shape[2]
    new_len = new_pages * PAGE
    first_slot = device_index * per_group

    def arrival_list():
        slot_ids = new_group * per_group + group_ranks(new_group)
        request_ids = jnp.arange(new_total, dtype=jnp.int32)
        return jnp.zeros((new_total,), jnp.int32).at[slot_ids].set(request_ids)

    def by_pieces():
        own_len = lax.dynamic_slice_in_dim(new_len, first_slot, per_group)
        arrival = arrival_list()
        older_rows = older_attention(ctx_len, queries, fresh_kv, cache_kv)
        return older_rows, exchange(
            prefill, prefill_scale, own_len, arrival, groups_count, per_group
        )

    if groups_count == 8 and per_group == 1 and prompt_len == LANES * PAGE:
        steps, local, slot_len, table = plan_routes(groups_count, new_group, new_pages, device_index)
        parts_count = lax.axis_size("parts")
        most = steps
        for shift in range(1, parts_count):
            there = [(p, (p + shift) % parts_count) for p in range(parts_count)]
            most = jnp.maximum(most, lax.ppermute(steps, "parts", there))
        choice = sum((most[0] > limit).astype(jnp.int32) for limit in STEP_CHOICES)
        resident = (ctx_len, queries, fresh_kv, cache_kv)
        branches = [
            functools.partial(handoff, limit, 1 + i, groups_count, local, table, prefill, prefill_scale, *resident)
            for i, limit in enumerate(STEP_CHOICES)
        ]
        older_rows, handed = lax.switch(choice, branches + [by_pieces])
    else:
        slot_len = lax.dynamic_slice_in_dim(new_len[arrival_list()], first_slot, per_group)
        older_rows, handed = by_pieces()
    return newer_attention(slot_len, queries, fresh_kv, older_rows, handed)


def solution(mesh):
    return jax.shard_map(
        on_device,
        mesh=mesh,
        in_specs=(
            P(("parts", "wide"), None, "tp"),
            P(None, ("parts", "wide"), None, "tp"),
            P(None, ("parts", "wide"), None, "tp"),
            P(("parts", "wide")),
            P(None, ("parts", "wide"), None, "tp"),
            P(None, ("parts", "wide"), None, "tp"),
            P("parts"),
            P("parts"),
        ),
        out_specs=(P(("parts", "wide"), None, "tp"), P(None, ("parts", "wide"), None, None, "tp")),
        check_vma=False,
    )
```

```python
import functools
import math

import jax
import jax.numpy as jnp
from jax import lax
from jax.experimental import pallas as pl
from jax.experimental.pallas import tpu as pltpu
from jax.sharding import PartitionSpec as P

HD = 128
PAGE = 16


NEG_FILL = -1e30


def group_ranks(groups):
    request_ids = jnp.arange(groups.shape[0], dtype=jnp.int32)
    earlier = (groups[None, :] == groups[:, None]) & (request_ids[None, :] < request_ids[:, None])
    return jnp.sum(earlier.astype(jnp.int32), axis=1)


def dequantize(values, scales):
    full_shape = values.shape
    widened = values.astype(jnp.float32).reshape(
        full_shape[:-1] + (scales.shape[-1], full_shape[-1] // scales.shape[-1])
    )
    return (
        (widened * scales.astype(jnp.float32)[..., None]).reshape(full_shape).astype(jnp.bfloat16)
    )


LANES = 128
DELAY = 5
SLOTS = 20
STEP_CHOICES = (124, 132, 140, 148, 156, 164, 172, 184, 204, 240)


def ring_position(index, n):
    odd = index % 2
    return (1 - odd) * (index // 2) + odd * (n - 1 - index // 2)


def ring_device(position, n):
    far = position // (n // 2)
    return (1 - far) * (2 * position) + far * (2 * (n - 1 - position) + 1)


def plan_kernel(n, group_ref, pages_ref, index_ref, steps_ref, local_ref, length_ref, table_ref):
    me = index_ref[0]
    order = [ring_device(p, n) for p in range(n)]
    pages = [pages_ref[d] for d in order]
    hops_forward = [(ring_position(group_ref[d], n) - p + n) % n for p, d in enumerate(order)]
    hops_backward = [(n - hops) % n for hops in hops_forward]
    count = 3**n
    rows = -(-count // (8 * LANES)) * 8
    number = lax.broadcasted_iota(jnp.int32, (rows, LANES), 0) * LANES + lax.broadcasted_iota(
        jnp.int32, (rows, LANES), 1
    )
    span = rows * LANES

    def shares(longer, p):
        moving = (hops_forward[p] > 0).astype(jnp.int32)
        near = (hops_forward[p] <= n // 2).astype(jnp.int32)
        ahead = moving * (near * (pages[p] - longer) + (1 - near) * longer)
        return ahead, moving * pages[p] - ahead

    def coarse(digit, p):
        return (pages[p] * digit) // 2

    def search(longer_of):
        rest = number
        forward, backward = [], []
        for p in range(n):
            third = (rest * 43691) >> 17
            digit = rest - 3 * third
            rest = third
            ahead, back = shares(longer_of(digit, p), p)
            forward.append(ahead)
            backward.append(back)
        needed = jnp.zeros((rows, LANES), jnp.int32)
        for e in range(n):
            for sent, hops, way in ((forward, hops_forward, 1), (backward, hops_backward, -1)):
                load = jnp.where(sent[e] > 0, jnp.maximum(hops[e] - 1, 0) * DELAY, 0)
                for p in range(n):
                    load = load + sent[p] * (((e - p) * way % n) < hops[p]).astype(jnp.int32)
                needed = jnp.maximum(needed, load)
        key = jnp.min((needed * span + number).astype(jnp.float32)).astype(jnp.int32)
        best = key % span
        longer = []
        for p in range(n):
            longer.append(longer_of(best % 3, p))
            best = best // 3
        return key // span, longer

    base = search(coarse)[1]

    def fine(digit, p):
        return jnp.clip(base[p] + (digit - 1) * (pages[p] // 8), 0, pages[p])

    steps, longer = search(fine)
    steps_ref[0] = steps
    sublane = lax.broadcasted_iota(jnp.int32, (8, LANES), 0)
    lane = lax.broadcasted_iota(jnp.int32, (8, LANES), 1)
    limits = jnp.zeros((8, LANES), jnp.int32)
    hops = limits
    firsts = limits
    for p in range(n):
        ahead, back = shares(longer[p], p)
        here = (sublane == 0) & (lane % n == p)
        there = (sublane == 1) & (lane % n == (n - p) % n)
        limits = jnp.where(here, ahead, jnp.where(there, back, limits))
        hops = jnp.where(here, hops_forward[p], jnp.where(there, hops_backward[p], hops))
        firsts = jnp.where(there, ahead, firsts)
    table_ref[0] = limits
    table_ref[1] = hops
    table_ref[2] = firsts
    local_ref[0] = (group_ref[me] == me).astype(jnp.int32)
    length = sum((group_ref[d] == me).astype(jnp.int32) * pages_ref[d] for d in range(n))
    local_ref[1] = length
    length_ref[0] = length * PAGE


def plan_routes(n, new_group, new_pages, device_index):
    return pl.pallas_call(
        functools.partial(plan_kernel, n),
        out_shape=(
            jax.ShapeDtypeStruct((1,), jnp.int32),
            jax.ShapeDtypeStruct((2,), jnp.int32),
            jax.ShapeDtypeStruct((1,), jnp.int32),
            jax.ShapeDtypeStruct((3, 8, LANES), jnp.int32),
        ),
        in_specs=[pl.BlockSpec(memory_space=pltpu.SMEM)] * 3,
        out_specs=(
            pl.BlockSpec(memory_space=pltpu.SMEM),
            pl.BlockSpec(memory_space=pltpu.SMEM),
            pl.BlockSpec(memory_space=pltpu.SMEM),
            pl.BlockSpec(memory_space=pltpu.VMEM),
        ),
    )(new_group, new_pages, device_index.reshape(1))


def attend_head(asked, own_key, own_value, keys, values, length):
    width = asked.shape[-1]
    grouped = jnp.concatenate([asked[:, at : at + HD] for at in range(0, width, HD)], axis=0)
    factor = 1.0 / math.sqrt(HD)
    scores = factor * lax.dot_general(
        grouped, keys, (((1,), (1,)), ((), ())), preferred_element_type=jnp.float32
    )
    usable = lax.broadcasted_iota(jnp.int32, scores.shape, 1) < length
    scores = jnp.where(usable, scores, NEG_FILL)
    own_score = factor * jnp.sum(
        grouped.astype(jnp.float32) * own_key.astype(jnp.float32), axis=1, keepdims=True
    )
    peak = jnp.maximum(jnp.max(scores, axis=1, keepdims=True), own_score)
    weights = jnp.where(usable, jnp.exp(scores - peak), 0.0)
    own_weight = jnp.exp(own_score - peak)
    total = jnp.sum(weights, axis=1, keepdims=True) + own_weight
    summed = jnp.dot(weights.astype(jnp.bfloat16), values, preferred_element_type=jnp.float32)
    own_rounded = own_weight.astype(jnp.bfloat16).astype(jnp.float32)
    summed = summed + own_rounded * own_value.astype(jnp.float32)
    result = (summed / total).astype(jnp.bfloat16)
    return jnp.concatenate([result[j : j + 1] for j in range(width // HD)], axis=1)


def older_kernel(length_ref, asked_ref, fresh_ref, cache_ref, out_ref):
    for r in range(out_ref.shape[0]):
        out_ref[r : r + 1, :] = attend_head(
            asked_ref[0, r : r + 1, :],
            fresh_ref[0, 0, r : r + 1, :],
            fresh_ref[1, 0, r : r + 1, :],
            cache_ref[0, r],
            cache_ref[1, r],
            length_ref[r],
        )


def older_attention(ctx_len, queries, fresh_kv, cache_kv):
    slots, width_asked = queries.shape[1:]
    resident_count, span_len, width = cache_kv.shape[1:]
    heads = width // HD
    asked = width_asked // heads
    return pl.pallas_call(
        older_kernel,
        grid=(heads,),
        out_shape=jax.ShapeDtypeStruct((resident_count, width_asked), jnp.bfloat16),
        in_specs=[
            pl.BlockSpec(memory_space=pltpu.SMEM),
            pl.BlockSpec((1, slots, asked), lambda h: (0, 0, h)),
            pl.BlockSpec((2, 1, slots, HD), lambda h: (0, 0, 0, h)),
            pl.BlockSpec((2, resident_count, span_len, HD), lambda h: (0, 0, 0, h)),
        ],
        out_specs=pl.BlockSpec((resident_count, asked), lambda h: (0, h)),
        compiler_params=pltpu.CompilerParams(vmem_limit_bytes=24 * 2**20),
    )(ctx_len, queries, fresh_kv, cache_kv)


def newer_kernel(length_ref, asked_ref, fresh_ref, older_ref, handed_ref, out_ref, kept_ref):
    kept_ref[...] = handed_ref[...]
    older = older_ref.shape[0]
    out_ref[0, :older, :] = older_ref[...]
    for r in range(handed_ref.shape[2]):
        out_ref[0, older + r : older + r + 1, :] = attend_head(
            asked_ref[0, older + r : older + r + 1, :],
            fresh_ref[0, 0, older + r : older + r + 1, :],
            fresh_ref[1, 0, older + r : older + r + 1, :],
            handed_ref[0, 0, r],
            handed_ref[1, 0, r],
            length_ref[r],
        )


def newer_attention(slot_len, queries, fresh_kv, older_rows, handed):
    slots, width_asked = queries.shape[1:]
    per_group, prompt_len, width = handed.shape[2:]
    heads = width // HD
    asked = width_asked // heads
    asked_spec = pl.BlockSpec((1, slots, asked), lambda h: (0, 0, h))
    handed_spec = pl.BlockSpec((2, 1, per_group, prompt_len, HD), lambda h: (0, 0, 0, 0, h))
    return pl.pallas_call(
        newer_kernel,
        grid=(heads,),
        out_shape=(
            jax.ShapeDtypeStruct(queries.shape, jnp.bfloat16),
            jax.ShapeDtypeStruct(handed.shape, jnp.bfloat16),
        ),
        in_specs=[
            pl.BlockSpec(memory_space=pltpu.SMEM),
            asked_spec,
            pl.BlockSpec((2, 1, slots, HD), lambda h: (0, 0, 0, h)),
            pl.BlockSpec((older_rows.shape[0], asked), lambda h: (0, h)),
            handed_spec,
        ],
        out_specs=(asked_spec, handed_spec),
        compiler_params=pltpu.CompilerParams(vmem_limit_bytes=24 * 2**20),
    )(slot_len, queries, fresh_kv, older_rows, handed)


def handoff_kernel(
    n, steps, local_ref, table_ref, prefill_ref, scale_ref,
    length_ref, asked_ref, fresh_ref, cache_ref, older_ref, out_ref,
    held, staged, hist, found, found_smem, send_sem, recv_sem, copy_sem,
):
    index = lax.axis_index("wide")
    place = ring_position(index, n)
    targets = (
        ring_device((place + 1) % n, n),
        ring_device((place + n - 1) % n, n),
    )
    barrier = pltpu.get_barrier_semaphore()
    for target in targets:
        pl.semaphore_signal(
            barrier, inc=1, device_id={"wide": target}, device_id_type=pl.DeviceIdType.MESH
        )
    pl.semaphore_wait(barrier, 2)

    pages = prefill_ref.shape[1]
    width = prefill_ref.shape[-1]
    heads = width // HD

    def widen(page):
        blocks = []
        for c in range(2):
            scale = scale_ref[c, page].astype(jnp.float32)
            values = prefill_ref[c, page].astype(jnp.float32)
            columns = [
                values[:, h * HD : (h + 1) * HD] * scale[:, h : h + 1] for h in range(heads)
            ]
            blocks.append(jnp.concatenate(columns, axis=1).astype(jnp.bfloat16))
        return blocks

    def keep_page(page):
        rows = pl.ds(pl.multiple_of(page * PAGE, PAGE), PAGE)
        for c, block in enumerate(widen(page)):
            out_ref[c, 0, 0, rows, :] = block

    sublane = lax.broadcasted_iota(jnp.int32, (8, LANES), 0)
    lane = lax.broadcasted_iota(jnp.int32, (8, LANES), 1)
    mirrored = (n - place) % n
    here = ((sublane == 0) & (lane == place)) | ((sublane == 1) & (lane == mirrored))
    limits = table_ref[0]
    hops = table_ref[1]
    firsts = table_ref[2]

    def arrivals(step, seen, to_go, page):
        landed = jnp.where(here & (to_go == 1), page + 1, 0)
        landed = jnp.sum(landed, axis=1, keepdims=True)
        return jnp.where(lane == landed - 1, step - DELAY, seen)

    def advance(step, sent, seen, first):
        if first:
            to_go = jnp.zeros((8, LANES), jnp.int32)
            page = to_go
        else:
            past = hist[step % DELAY]
            past = pltpu.roll(past, 1, 1)
            to_go = past % 16
            page = past // 16
            seen = arrivals(step, seen, to_go, page)
        forwards = to_go > 1
        injects = jnp.logical_not(forwards) & (sent < limits)
        now = jnp.where(forwards, page * 16 + to_go - 1, jnp.where(injects, (firsts + sent) * 16 + hops, 0))
        hist[step % DELAY] = now
        code = jnp.where(here, jnp.where(forwards, pages, jnp.where(injects, firsts + sent, 0)), 0)
        codes = (
            jnp.sum(jnp.where(sublane == 0, code, 0)),
            jnp.sum(jnp.where(sublane == 1, code, 0)),
        )
        return sent + injects.astype(jnp.int32), seen, codes

    def hop(step, way):
        return pltpu.make_async_remote_copy(
            src_ref=staged.at[way, step % SLOTS],
            dst_ref=held.at[way, step],
            send_sem=send_sem.at[way, step % SLOTS],
            recv_sem=recv_sem.at[way, step % SLOTS],
            device_id={"wide": targets[way]},
            device_id_type=pl.DeviceIdType.MESH,
        )

    def one_step(step, carry, first, reuse):
        sent, seen = carry
        sent, seen, codes = advance(step, sent, seen, first)
        for way in range(2):
            if reuse:
                hop(step - SLOTS, way).wait_send()
            mine = widen(jnp.minimum(codes[way], pages - 1))
            if not first:
                hop(step - DELAY, way).wait_recv()
            for c in range(2):
                block = mine[c]
                if not first:
                    block = jnp.where(codes[way] >= pages, held[way, step - DELAY, c], block)
                staged[way, step % SLOTS, c] = block
            hop(step, way).start()
        keep_page(step % pages)
        return sent, seen

    carry = (jnp.zeros((8, LANES), jnp.int32), jnp.full((8, LANES), -1, jnp.int32))
    carry = lax.fori_loop(0, DELAY, lambda t, c: one_step(t, c, True, False), carry)
    carry = lax.fori_loop(DELAY, SLOTS, lambda t, c: one_step(t, c, False, False), carry)
    resident_count = cache_ref.shape[1]
    asked = asked_ref.shape[-1] // heads
    between = (steps - SLOTS) // (heads + 1)

    def attend_older(head):
        columns = pl.ds(pl.multiple_of(head * HD, HD), HD)
        outer = pl.ds(pl.multiple_of(head * asked, asked), asked)
        for r in range(resident_count):
            older_ref[r : r + 1, outer] = attend_head(
                asked_ref[0, r : r + 1, outer],
                fresh_ref[0, 0, r : r + 1, columns],
                fresh_ref[1, 0, r : r + 1, columns],
                cache_ref[0, r, :, columns],
                cache_ref[1, r, :, columns],
                length_ref[r],
            )

    def stretch(head, carry):
        start = SLOTS + head * between
        carry = lax.fori_loop(
            start, start + between, lambda t, c: one_step(t, c, False, True), carry
        )
        attend_older(head)
        return carry

    carry = lax.fori_loop(0, heads, stretch, carry)
    carry = lax.fori_loop(
        SLOTS + heads * between, steps, lambda t, c: one_step(t, c, False, True), carry
    )
    sent, seen = carry

    def keep_late(page, carry):
        keep_page(page)
        return carry

    lax.fori_loop(min(steps, pages), pages, keep_late, 0)

    def settle(step, seen):
        past = pltpu.roll(hist[step % DELAY], 1, 1)
        for way in range(2):
            hop(step - DELAY, way).wait_recv()
        return arrivals(step, seen, past % 16, past // 16)

    seen = lax.fori_loop(steps, steps + DELAY, settle, seen)

    def drain(step, carry):
        for way in range(2):
            hop(step, way).wait_send()
        return carry

    lax.fori_loop(steps - SLOTS, steps, drain, 0)

    found[...] = seen
    fetch = pltpu.make_async_copy(found, found_smem, copy_sem)
    fetch.start()
    fetch.wait()

    stays = local_ref[0]
    length = local_ref[1]

    def place_page(page, carry):
        forward = found_smem[0, page]
        backward = found_smem[1, page]
        from_backward = (backward >= 0).astype(jnp.int32)
        at = jnp.where(from_backward == 1, backward, jnp.maximum(forward, 0))
        rows = pl.ds(pl.multiple_of(page * PAGE, PAGE), PAGE)
        for c in range(2):
            block = jnp.where(stays == 1, out_ref[c, 0, 0, rows, :], held[from_backward, at, c])
            out_ref[c, 0, 0, rows, :] = jnp.where(page < length, block, jnp.zeros_like(block))
        return carry

    lax.fori_loop(0, pages, place_page, 0)


def handoff(
    steps, collective_id, n, local, table, prefill, prefill_scale,
    ctx_len, queries, fresh_kv, cache_kv,
):
    prompt_len, width = prefill.shape[2:]
    return pl.pallas_call(
        functools.partial(handoff_kernel, n, steps),
        out_shape=(
            jax.ShapeDtypeStruct((cache_kv.shape[1], queries.shape[2]), jnp.bfloat16),
            jax.ShapeDtypeStruct((2, 1, 1, prompt_len, width), jnp.bfloat16),
        ),
        in_specs=[pl.BlockSpec(memory_space=pltpu.SMEM)]
        + [pl.BlockSpec(memory_space=pltpu.VMEM)] * 3
        + [pl.BlockSpec(memory_space=pltpu.SMEM)]
        + [pl.BlockSpec(memory_space=pltpu.VMEM)] * 3,
        out_specs=(pl.BlockSpec(memory_space=pltpu.VMEM),) * 2,
        scratch_shapes=[
            pltpu.VMEM((2, steps, 2, PAGE, width), jnp.bfloat16),
            pltpu.VMEM((2, SLOTS, 2, PAGE, width), jnp.bfloat16),
            pltpu.VMEM((DELAY, 8, LANES), jnp.int32),
            pltpu.VMEM((8, LANES), jnp.int32),
            pltpu.SMEM((8, LANES), jnp.int32),
            pltpu.SemaphoreType.DMA((2, SLOTS)),
            pltpu.SemaphoreType.DMA((2, SLOTS)),
            pltpu.SemaphoreType.DMA,
        ],
        compiler_params=pltpu.CompilerParams(
            collective_id=collective_id, has_side_effects=True, vmem_limit_bytes=50 * 2**20
        ),
    )(
        local,
        table,
        prefill.reshape(2, -1, PAGE, width),
        prefill_scale.reshape(2, -1, PAGE, width // HD),
        ctx_len,
        queries,
        fresh_kv,
        cache_kv,
    )


def exchange(prefill, prefill_scale, own_len, arrival, groups_count, per_group):
    prompt_len, width_here = prefill.shape[2:]
    positions = jnp.arange(prompt_len, dtype=jnp.int32)
    local_kv = dequantize(prefill, prefill_scale)
    keeping = positions[None, :] < own_len[:, None]
    local_kv = jnp.where(keeping[None, :, :, None], local_kv, jnp.zeros((), jnp.bfloat16))
    split_kv = local_kv.reshape(2, per_group, groups_count, prompt_len // groups_count, width_here)
    held = lax.all_to_all(split_kv, "wide", split_axis=2, concat_axis=1, tiled=True)
    ordered = held[:, arrival]
    return lax.all_to_all(ordered, "wide", split_axis=1, concat_axis=3, tiled=True)


def on_device(queries, cache_kv, fresh_kv, ctx_len, prefill, prefill_scale, new_group, new_pages):
    groups_count = lax.axis_size("wide")
    device_index = lax.axis_index("wide")
    new_total = new_group.shape[0]
    per_group = new_total // groups_count
    prompt_len = prefill.shape[2]
    new_len = new_pages * PAGE
    first_slot = device_index * per_group

    def arrival_list():
        slot_ids = new_group * per_group + group_ranks(new_group)
        request_ids = jnp.arange(new_total, dtype=jnp.int32)
        return jnp.zeros((new_total,), jnp.int32).at[slot_ids].set(request_ids)

    def by_pieces():
        own_len = lax.dynamic_slice_in_dim(new_len, first_slot, per_group)
        arrival = arrival_list()
        older_rows = older_attention(ctx_len, queries, fresh_kv, cache_kv)
        return older_rows, exchange(
            prefill, prefill_scale, own_len, arrival, groups_count, per_group
        )

    if groups_count == 8 and per_group == 1 and prompt_len == LANES * PAGE:
        steps, local, slot_len, table = plan_routes(groups_count, new_group, new_pages, device_index)
        parts_count = lax.axis_size("parts")
        most = steps
        for shift in range(1, parts_count):
            there = [(p, (p + shift) % parts_count) for p in range(parts_count)]
            most = jnp.maximum(most, lax.ppermute(steps, "parts", there))
        choice = sum((most[0] > limit).astype(jnp.int32) for limit in STEP_CHOICES)
        resident = (ctx_len, queries, fresh_kv, cache_kv)
        branches = [
            functools.partial(handoff, limit, 1 + i, groups_count, local, table, prefill, prefill_scale, *resident)
            for i, limit in enumerate(STEP_CHOICES)
        ]
        older_rows, handed = lax.switch(choice, branches + [by_pieces])
    else:
        slot_len = lax.dynamic_slice_in_dim(new_len[arrival_list()], first_slot, per_group)
        older_rows, handed = by_pieces()
    return newer_attention(slot_len, queries, fresh_kv, older_rows, handed)


def solution(mesh):
    return jax.shard_map(
        on_device,
        mesh=mesh,
        in_specs=(
            P(("parts", "wide"), None, "tp"),
            P(None, ("parts", "wide"), None, "tp"),
            P(None, ("parts", "wide"), None, "tp"),
            P(("parts", "wide")),
            P(None, ("parts", "wide"), None, "tp"),
            P(None, ("parts", "wide"), None, "tp"),
            P("parts"),
            P("parts"),
        ),
        out_specs=(P(("parts", "wide"), None, "tp"), P(None, ("parts", "wide"), None, None, "tp")),
        check_vma=False,
    )
```
